256 devices in a mesh: row: 16 (over z_hi, y, core), col: 16 (over z_lo, x).
Axes of the slice: x: 4, y: 4, z: 8 (z_hi: 2, z_lo: 4; z = z_hi * 4 + z_lo), core: 2. Of those that a mesh axis runs over, the one named last changes fastest.
Arguments:
- vectors: float32 [4, 16, 16, 16, 128], P(None, 'col', 'row'), may hold values from -6 to 6
- tiles: float32 [16, 16, 96, 128, 128], P('row', 'col')
- tile_rows: int32 [16, 16, 96], P('row', 'col'), may hold values from 0 to 63, as said below
- tile_cols: int32 [16, 16, 96], P('row', 'col'), may hold values from 0 to 63
- counts: int32 [16, 16], P('row', 'col'), may hold values from 1 to 96
Outputs:
- product: float32 [4, 16, 16, 16, 128], P(None, 'col', 'row')
The draws below stay inside these ranges and needn't reach their ends.
Inputs may be any that keep to these rules, and one draw needn't show every extreme that they name: `tile_rows`: live slots have i_s <= j_s, and no pair (i_s, j_s) is named by two live slots of the whole array.
All inputs are finite; a program needn't handle non-finite values.
Results may differ from the reference program's by a relative error of at most 0.0003.
Values sent between devices are 32-bit elements; how exact they have to be, the bound alone decides.
No kernel may reach another device: no remote copies, remote signals or barrier semaphores. Data moves between devices by JAX's collectives and lax.ppermute only.
A program may use at most 64 MiB of HBM per device.

```python
import math
import jax
import jax.numpy as jnp
from jax import lax

TS = 128
VECS = 16
NA = 4
TMAX = 96
N_ROW = 16
N_COL = 16


def tile_pattern(key):
    row_tiles = NA * N_COL
    col_tiles = NA * N_ROW
    pair_total = row_tiles * col_tiles
    row_axis = jnp.arange(N_ROW, dtype=jnp.int32)[:, None, None, None]
    col_axis = jnp.arange(N_COL, dtype=jnp.int32)[None, :, None, None]
    local_row = jnp.arange(row_tiles, dtype=jnp.int32)[None, None, :, None]
    local_col = jnp.arange(col_tiles, dtype=jnp.int32)[None, None, None, :]
    global_row = local_row * N_ROW + row_axis
    global_col = (local_col // N_ROW * N_COL + col_axis) * N_ROW + local_col % N_ROW
    upper_pair = global_row <= global_col
    pair_ids = local_row * col_tiles + local_col
    noise_bits = jax.random.randint(jax.random.fold_in(key, 101), (N_ROW, N_COL, row_tiles, col_tiles), 0, max(2, 2 ** 30 // pair_total))
    scores = jnp.where(upper_pair, noise_bits * pair_total + pair_ids, -1 - pair_ids).reshape(N_ROW, N_COL, pair_total)
    chosen = lax.top_k(scores, TMAX)[1].astype(jnp.int32)
    slot_rows = (chosen // col_tiles).astype(jnp.int32)
    slot_cols = (chosen % col_tiles).astype(jnp.int32)
    available = jnp.sum(upper_pair.astype(jnp.int32), axis=(2, 3))
    drawn_count = jax.random.randint(jax.random.fold_in(key, 102), (N_ROW, N_COL), max(1, TMAX // 4), TMAX + 1)
    device_order = jax.random.permutation(jax.random.fold_in(key, 103), N_ROW * N_COL).reshape(N_ROW, N_COL).astype(jnp.int32)
    ranked = jnp.where(available >= TMAX, device_order, -1)
    target = jnp.argmax(ranked.reshape(-1)).astype(jnp.int32)
    flat_ids = jnp.arange(N_ROW * N_COL, dtype=jnp.int32).reshape(N_ROW, N_COL)
    counts = jnp.where(flat_ids == target, TMAX, jnp.minimum(drawn_count, available)).astype(jnp.int32)
    return (slot_rows, slot_cols, counts)


def draw_tile_rows(key, part):
    slot_rows, slot_cols, counts = tile_pattern(key)
    return slot_rows


def draw_tile_cols(key, part):
    slot_rows, slot_cols, counts = tile_pattern(key)
    return slot_cols


def draw_counts(key, part):
    slot_rows, slot_cols, counts = tile_pattern(key)
    return counts


def draw_tiles(key, part):
    slot_rows, slot_cols, counts = tile_pattern(key)
    key = jax.random.fold_in(key, 4)
    row_axis = jnp.arange(N_ROW, dtype=jnp.int32)[:, None, None]
    col_axis = jnp.arange(N_COL, dtype=jnp.int32)[None, :, None]
    global_row = slot_rows * N_ROW + row_axis
    global_col = (slot_cols // N_ROW * N_COL + col_axis) * N_ROW + slot_cols % N_ROW
    diagonal = (global_row == global_col)[..., None, None]
    tile_scale = 1.0 / math.sqrt(TMAX * TS / NA)
    full_shape = (N_ROW, N_COL, TMAX, TS, TS)
    values = jax.random.normal(key, full_shape, jnp.float32)
    values = jnp.where(diagonal, 0.5 * (values + jnp.swapaxes(values, 3, 4)), values)
    return values * tile_scale


def block_scale(key, extent, shards, least, high):
    loudness, own = 1.0, jax.random.fold_in(key, 6)
    for dim, blocks in shards:
        heights = jnp.exp(jax.random.uniform(jax.random.fold_in(own, dim), (blocks,), jnp.float32, least / len(shards), high / len(shards)))
        loudness = loudness * jnp.repeat(heights, extent[dim] // blocks).reshape([-1 if axis == dim else 1 for axis in range(len(extent))])
    return loudness


def noise(stream_key, extent, scale, reach, split=(), kind=jnp.bfloat16):
    values = jax.random.normal(stream_key, extent, jnp.float32) * scale
    if len(split) > 0:
        values = block_scale(stream_key, extent, split, -0.22, 0.18) * values
    return jnp.clip(values, min=-reach, max=reach).astype(kind)


def setup_inputs(seed: int = 0) -> dict:
    seeds = jax.random.split(jax.random.key(seed), 6)
    return {
        "vectors": noise(seeds[0], (NA, N_COL, N_ROW, VECS, TS), 1.0, 6.0, ((1, 16), (2, 16)), jnp.float32),
        "tiles": draw_tiles(jax.random.fold_in(seeds[5], 71), 0),
        "tile_rows": draw_tile_rows(jax.random.fold_in(seeds[5], 71), 0),
        "tile_cols": draw_tile_cols(jax.random.fold_in(seeds[5], 71), 0),
        "counts": draw_counts(jax.random.fold_in(seeds[5], 71), 0),
    }


def reference(vectors, tiles, tile_rows, tile_cols, counts):
    total_tiles = NA * N_ROW * N_COL
    flat_vectors = vectors.reshape(total_tiles, VECS, TS)
    slot_ids = jnp.arange(TMAX, dtype=jnp.int32)

    def device_step(result, inputs):
        block_tiles, rows_local, cols_local, live_count, row_index, col_index = inputs
        live_mask = slot_ids < live_count
        global_row = (rows_local * N_ROW + row_index).astype(jnp.int32)
        global_col = (((cols_local // N_ROW) * N_COL + col_index) * N_ROW + cols_local % N_ROW).astype(jnp.int32)
        mirror = live_mask & (global_row < global_col)
        picked_cols = flat_vectors[global_col]
        picked_rows = flat_vectors[global_row]
        forward = jnp.einsum("skm,svm->svk", block_tiles, picked_cols, precision=lax.Precision.HIGHEST)
        backward = jnp.einsum("skm,svk->svm", block_tiles, picked_rows, precision=lax.Precision.HIGHEST)
        forward = jnp.where(live_mask[:, None, None], forward, 0.0)
        backward = jnp.where(mirror[:, None, None], backward, 0.0)
        result = result.at[global_row].add(forward)
        result = result.at[global_col].add(backward)
        return result, None

    row_ids = jnp.repeat(jnp.arange(N_ROW, dtype=jnp.int32), N_COL)
    col_ids = jnp.tile(jnp.arange(N_COL, dtype=jnp.int32), N_ROW)
    inputs = (tiles.reshape(N_ROW * N_COL, TMAX, TS, TS), tile_rows.reshape(N_ROW * N_COL, TMAX),
              tile_cols.reshape(N_ROW * N_COL, TMAX), counts.reshape(N_ROW * N_COL), row_ids, col_ids)
    result, _ = lax.scan(device_step, jnp.zeros((total_tiles, VECS, TS), jnp.float32), inputs)
    return result.reshape(NA, N_COL, N_ROW, VECS, TS)
```

```python
import jax
import jax.numpy as jnp
from jax import lax
from jax.sharding import PartitionSpec as P


def exchange(parts, axis):
    return lax.all_to_all(parts, axis, 0, 0, tiled=True)


def shards(vectors, tiles, tile_rows, tile_cols, counts):
    row_count = lax.axis_size("row")
    col_count = lax.axis_size("col")
    row_index = lax.axis_index("row")
    col_index = lax.axis_index("col")
    blocks = vectors.shape[0]
    vec_count = vectors.shape[3]
    tile_edge = vectors.shape[4]
    slot_count = tiles.shape[2]
    local_rows = blocks * col_count
    local_cols = blocks * row_count
    own = vectors.reshape(1, blocks, vec_count, tile_edge)
    column_side = exchange(jnp.tile(own, (row_count, 1, 1, 1)), "row").reshape(
        local_cols, vec_count, tile_edge
    )
    row_side = exchange(jnp.tile(own, (col_count, 1, 1, 1)), "col").reshape(
        local_rows, vec_count, tile_edge
    )
    block_tiles = tiles.reshape(slot_count, tile_edge, tile_edge)
    rows_local = tile_rows.reshape(slot_count)
    cols_local = tile_cols.reshape(slot_count)
    live_count = counts.reshape(())
    slot_ids = jnp.arange(slot_count, dtype=jnp.int32)
    live_mask = slot_ids < live_count
    global_row = rows_local * row_count + row_index
    global_col = (
        cols_local // row_count * col_count + col_index
    ) * row_count + cols_local % row_count
    mirror = live_mask & (global_row < global_col)
    row_key = rows_local % col_count * blocks + rows_local // col_count
    col_key = cols_local % row_count * blocks + cols_local // row_count
    picked_cols = jnp.take(column_side, col_key, axis=0)
    picked_rows = jnp.take(row_side, row_key, axis=0)
    forward = jnp.einsum(
        "skm,svm->svk",
        block_tiles,
        picked_cols,
        precision=lax.Precision.HIGHEST,
        preferred_element_type=jnp.float32,
    )
    backward = jnp.einsum(
        "skm,svk->svm",
        block_tiles,
        picked_rows,
        precision=lax.Precision.HIGHEST,
        preferred_element_type=jnp.float32,
    )
    forward = jnp.where(live_mask[:, None, None], forward, 0.0).reshape(
        slot_count, vec_count * tile_edge
    )
    backward = jnp.where(mirror[:, None, None], backward, 0.0).reshape(
        slot_count, vec_count * tile_edge
    )
    targets = jnp.arange(lax.axis_size("col") * blocks, dtype=jnp.int32)
    onehot = (targets[:, None] == row_key[None, :]).astype(jnp.float32)
    row_part = exchange(
        jnp.dot(
            onehot, forward, precision=lax.Precision.HIGHEST, preferred_element_type=jnp.float32
        ).reshape(col_count, blocks, vec_count, tile_edge),
        "col",
    ).sum(0)
    targets = jnp.arange(lax.axis_size("row") * blocks, dtype=jnp.int32)
    onehot = (targets[:, None] == col_key[None, :]).astype(jnp.float32)
    col_part = exchange(
        jnp.dot(
            onehot, backward, precision=lax.Precision.HIGHEST, preferred_element_type=jnp.float32
        ).reshape(row_count, blocks, vec_count, tile_edge),
        "row",
    ).sum(0)
    return (row_part + col_part).reshape(blocks, 1, 1, vec_count, tile_edge)


def solution(mesh):
    in_specs = (
        P(None, "col", "row", None, None),
        P("row", "col", None, None, None),
        P("row", "col", None),
        P("row", "col", None),
        P("row", "col"),
    )
    out_specs = P(None, "col", "row", None, None)
    return jax.shard_map(shards, mesh=mesh, in_specs=in_specs, out_specs=out_specs, check_vma=False)
```

```python
import functools
import jax
import jax.numpy as jnp
from jax import lax
from jax.experimental import pallas as pl
from jax.experimental.pallas import tpu as pltpu
from jax.sharding import PartitionSpec as P

AXIS = 16
GROUP = 4
CHUNK = 8
BF16 = jnp.bfloat16
F32 = jnp.float32


def send(value, axis, target):
    return lax.ppermute(value, axis, [(i, target(i)) for i in range(AXIS)])


def turn_y(step):
    return lambda i: i // 8 * 8 + (i // 2 + step) % 4 * 2 + i % 2


def turn_x(step):
    return lambda i: i // 4 * 4 + (i + step) % 4


def turn_z(step):
    return lambda i: (i + 4 * step) % AXIS


def other_z(i):
    return i ^ 8


def other_core(i):
    return i ^ 1


def multiply_kernel(transposed, part_count, out_count, *refs):
    source, target, live = refs[:3]
    parts = refs[3 : 3 + part_count]
    tiles = refs[3 + part_count]
    outs = refs[4 + part_count : 4 + part_count + out_count]
    split, total, held, arrived = refs[4 + part_count + out_count :]
    chunks = held.shape[0] // CHUNK
    vecs = split.shape[1] // 2
    edge = split.shape[2] // 2

    def fetch(chunk):
        span = pl.ds(chunk * CHUNK, CHUNK)
        return pltpu.make_async_copy(tiles.at[span], held.at[span], arrived.at[chunk])

    for chunk in range(chunks):
        fetch(chunk).start()
    place = 0
    for part in parts:
        values = part[...]
        high = values.astype(BF16)
        low = (values - high.astype(F32)).astype(BF16)
        span = slice(place, place + part.shape[0])
        split[span, :vecs, :edge] = high
        split[span, :vecs, edge:] = high
        split[span, vecs:, :edge] = low
        split[span, vecs:, edge:] = low
        place += part.shape[0]
    total[...] = jnp.zeros_like(total)

    def one_slot(slot):
        tile = held[slot]
        high = tile.astype(BF16)
        low = (tile - high.astype(F32)).astype(BF16)
        both = jnp.concatenate([high, low], axis=0 if transposed else 1)
        product = lax.dot_general(
            split[source[slot]],
            both,
            (((1,), (0 if transposed else 1,)), ((), ())),
            preferred_element_type=F32,
        )
        total[target[slot]] += product[:vecs] + product[vecs:]

    def one_chunk(chunk, carry):
        fetch(chunk).wait()

        @pl.when(chunk * CHUNK < live[0])
        def _():
            for step in range(CHUNK):
                one_slot(chunk * CHUNK + step)

        return carry

    lax.fori_loop(0, chunks, one_chunk, 0)
    place = 0
    for out in outs:
        out[...] = total[place : place + out.shape[0]]
        place += out.shape[0]


def multiply(transposed, source, target, live, parts, tiles, out_count):
    slots, edge = tiles.shape[0], tiles.shape[1]
    vecs = parts[0].shape[1]
    places = sum(part.shape[0] for part in parts)
    scalars = [pl.BlockSpec(memory_space=pltpu.SMEM)] * 3
    vector = pl.BlockSpec(memory_space=pltpu.VMEM)
    return pl.pallas_call(
        functools.partial(multiply_kernel, transposed, len(parts), out_count),
        out_shape=[jax.ShapeDtypeStruct((places // out_count, vecs, edge), F32)] * out_count,
        in_specs=scalars + [vector] * len(parts) + [pl.BlockSpec(memory_space=pl.ANY)],
        out_specs=[vector] * out_count,
        scratch_shapes=[
            pltpu.VMEM((places, 2 * vecs, 2 * edge), BF16),
            pltpu.VMEM((places + 8, vecs, edge), F32),
            pltpu.VMEM((slots, edge, edge), F32),
            pltpu.SemaphoreType.DMA((slots // CHUNK,)),
        ],
        compiler_params=pltpu.CompilerParams(vmem_limit_bytes=20 * 1024 * 1024),
        cost_estimate=pl.CostEstimate(
            flops=8 * slots * vecs * edge * edge, bytes_accessed=4 * slots * edge * edge, transcendentals=0
        ),
        name="backward" if transposed else "forward",
    )(source, target, live, *parts, tiles)


def shards(vectors, tiles, tile_rows, tile_cols, counts):
    blocks = vectors.shape[0]
    vecs, edge = vectors.shape[3], vectors.shape[4]
    slots = tiles.shape[2]
    row, col = lax.axis_index("row"), lax.axis_index("col")
    tiles = tiles.reshape(slots, edge, edge)
    rows, cols = tile_rows.reshape(slots), tile_cols.reshape(slots)
    live = counts.reshape(1)
    row_block, row_col = rows // AXIS, rows % AXIS
    col_block, col_row = cols // AXIS, cols % AXIS
    is_live = jnp.arange(slots, dtype=jnp.int32) < live
    mirror = is_live & (rows * AXIS + row < (col_block * AXIS + col) * AXIS + col_row)

    def row_place(step_y):
        core, z = (col_row ^ row) & 1, (col_row ^ row) >> 3
        return ((core * GROUP + (step_y & 3)) * 2 + z) * blocks + col_block

    def col_place(step_x, step_z):
        return ((step_x & 3) * GROUP + (step_z & 3)) * blocks + row_block

    nowhere = blocks * AXIS
    step_y = (col_row >> 1) - (row >> 1)
    step_x, step_z = row_col - col, (row_col >> 2) - (col >> 2)
    forward_source = row_place(-step_y)
    forward_target = jnp.where(is_live, col_place(step_x, step_z), nowhere)
    backward_source = col_place(-step_x, -step_z)
    backward_target = jnp.where(mirror, row_place(step_y), nowhere)

    own = vectors.reshape(blocks, vecs, edge)
    with jax.named_scope("gather_z"):
        across = send(own, "row", other_z)
        along = [send(own, "col", turn_z(step)) for step in (1, 2, 3)]
    with jax.named_scope("gather_y"):
        pair = jnp.concatenate([own, across])
        sides = [pair] + [send(pair, "row", turn_y(step)) for step in (1, 2, 3)]
    with jax.named_scope("gather_core"):
        sides = sides + [send(side, "row", other_core) for side in sides]
    with jax.named_scope("gather_x"):
        line = jnp.concatenate([own] + along)
        lines = [line] + [send(line, "col", turn_x(step)) for step in (1, 2, 3)]
    row_parts = multiply(False, forward_source, forward_target, live, sides, tiles, 4)
    col_parts = multiply(True, backward_source, backward_target, live, lines, tiles, 2)
    with jax.named_scope("sum_x"):
        line = row_parts[0]
        for step in (1, 2, 3):
            line = line + send(row_parts[step], "col", turn_x(step))
    with jax.named_scope("sum_core"):
        side = col_parts[0] + send(col_parts[1], "row", other_core)
    with jax.named_scope("sum_y"):
        side = side.reshape(GROUP, 2 * blocks, vecs, edge)
        pair = side[0]
        for step in (1, 2, 3):
            pair = pair + send(side[step], "row", turn_y(step))
    with jax.named_scope("sum_z"):
        line = line.reshape(GROUP, blocks, vecs, edge)
        result = line[0] + pair[:blocks] + send(pair[blocks:], "row", other_z)
        for step in (1, 2, 3):
            result = result + send(line[step], "col", turn_z(step))
    return result.reshape(blocks, 1, 1, vecs, edge)


def solution(mesh):
    in_specs = (
        P(None, "col", "row", None, None),
        P("row", "col", None, None, None),
        P("row", "col", None),
        P("row", "col", None),
        P("row", "col"),
    )
    out_specs = P(None, "col", "row", None, None)
    return jax.shard_map(shards, mesh=mesh, in_specs=in_specs, out_specs=out_specs, check_vma=False)
```

```python
import functools
import jax
import jax.numpy as jnp
from jax import lax
from jax.experimental import pallas as pl
from jax.experimental.pallas import tpu as pltpu
from jax.sharding import PartitionSpec as P

AXIS = 16
GROUP = 4
CHUNK = 8
BF16 = jnp.bfloat16
F32 = jnp.float32
AXES = ("row", "col")


def send(value, target):
    pairs = []
    for row in range(AXIS):
        for col in range(AXIS):
            place = target(row, col)
            if place is not None:
                pairs.append((row * AXIS + col, place[0] * AXIS + place[1]))
    return lax.ppermute(value, AXES, pairs)


def to_other_core(row, col):
    return row ^ 1, col


def along_z(step):
    def target(row, col):
        if row % 2 == 1:
            return row, (col + 4 * step) % AXIS
        return (row ^ 8, col) if step == 1 else None

    return target


def along_side(step):
    def target(row, col):
        if row % 2 == 1:
            return row, col // 4 * 4 + (col + step) % 4
        return row // 8 * 8 + (row // 2 + step) % 4 * 2, col

    return target


def multiply_kernel(held, *refs):
    core, source, target, live = refs[:4]
    parts = refs[4:8]
    tiles = refs[8]
    outs = refs[9:13]
    split, total, block, arrived = refs[13:]
    chunks = block.shape[0] // CHUNK
    vecs = split.shape[1] // 2
    edge = split.shape[2] // 2
    count = outs[0].shape[0]
    blocks = count // GROUP

    def fetch(chunk):
        span = pl.ds(chunk * CHUNK, CHUNK)
        return pltpu.make_async_copy(tiles.at[span], block.at[span], arrived.at[chunk])

    for chunk in range(chunks):
        fetch(chunk).start()

    def put(place, values):
        high = values.astype(BF16)
        low = (values - high.astype(F32)).astype(BF16)
        span = slice(place, place + values.shape[0])
        split[span, :vecs, :edge] = high
        split[span, :vecs, edge:] = high
        split[span, vecs:, :edge] = low
        split[span, vecs:, edge:] = low

    def one_slot(transposed, slot):
        tile = block[slot]
        high = tile.astype(BF16)
        low = (tile - high.astype(F32)).astype(BF16)
        both = jnp.concatenate([high, low], axis=0 if transposed else 1)
        product = lax.dot_general(
            split[source[slot]],
            both,
            (((1,), (0 if transposed else 1,)), ((), ())),
            preferred_element_type=F32,
        )
        total[target[slot]] += product[:vecs] + product[vecs:]

    def run(transposed):
        def one_chunk(chunk, carry):
            fetch(chunk).wait()

            @pl.when(chunk * CHUNK < live[0])
            def _():
                for step in range(CHUNK):
                    one_slot(transposed, chunk * CHUNK + step)

            return carry

        lax.fori_loop(0, chunks, one_chunk, 0)

    total[...] = jnp.zeros_like(total)

    @pl.when(core[0] == 0)
    def _():
        for index, part in enumerate(parts):
            put(index * count, part[:count])
        run(not held)

    @pl.when(core[0] != 0)
    def _():
        for index, part in enumerate(parts):
            if held:
                for step in range(GROUP):
                    span = slice(2 * step * blocks, (2 * step + 1) * blocks)
                    put(index * count + step * blocks, part[span])
            else:
                put(index * count, part[...])
        run(held)

    for index, out in enumerate(outs):
        out[...] = total[index * count : (index + 1) * count]


def multiply(held, core, source, target, live, parts, tiles):
    slots, edge = tiles.shape[0], tiles.shape[1]
    vecs = parts[0].shape[1]
    count = parts[0].shape[0] // (2 if held else 1)
    places = GROUP * count
    scalars = [pl.BlockSpec(memory_space=pltpu.SMEM)] * 4
    vector = pl.BlockSpec(memory_space=pltpu.VMEM)
    return pl.pallas_call(
        functools.partial(multiply_kernel, held),
        out_shape=[jax.ShapeDtypeStruct((count, vecs, edge), F32)] * GROUP,
        in_specs=scalars + [vector] * GROUP + [pl.BlockSpec(memory_space=pl.ANY)],
        out_specs=[vector] * GROUP,
        scratch_shapes=[
            pltpu.VMEM((places, 2 * vecs, 2 * edge), BF16),
            pltpu.VMEM((places + 8, vecs, edge), F32),
            pltpu.VMEM((slots, edge, edge), F32),
            pltpu.SemaphoreType.DMA((slots // CHUNK,)),
        ],
        compiler_params=pltpu.CompilerParams(vmem_limit_bytes=20 * 1024 * 1024),
        cost_estimate=pl.CostEstimate(
            flops=8 * slots * vecs * edge * edge, bytes_accessed=4 * slots * edge * edge, transcendentals=0
        ),
        name="first" if held else "second",
    )(core, source, target, live, *parts, tiles)


def merge_kernel(core, *refs):
    kept, got, outs = refs[:4], refs[4:8], refs[8:12]
    count = kept[0].shape[0]
    blocks = count // GROUP

    @pl.when(core[0] == 0)
    def _():
        for index in range(GROUP):
            outs[index][:count] = kept[index][...] + got[index][...]
            outs[index][count:] = jnp.zeros_like(got[index])

    @pl.when(core[0] != 0)
    def _():
        for index in range(GROUP):
            for step in range(GROUP):
                span = slice(step * blocks, (step + 1) * blocks)
                low = 2 * step * blocks
                outs[index][low : low + blocks] = kept[index][span]
                outs[index][low + blocks : low + 2 * blocks] = got[index][span]


def merge(core, kept, got):
    count, vecs, edge = kept[0].shape
    vector = pl.BlockSpec(memory_space=pltpu.VMEM)
    return pl.pallas_call(
        merge_kernel,
        out_shape=[jax.ShapeDtypeStruct((2 * count, vecs, edge), F32)] * GROUP,
        in_specs=[pl.BlockSpec(memory_space=pltpu.SMEM)] + [vector] * (2 * GROUP),
        out_specs=[vector] * GROUP,
        compiler_params=pltpu.CompilerParams(vmem_limit_bytes=8 * 1024 * 1024),
        name="merge",
    )(core, *kept, *got)


def shards(vectors, tiles, tile_rows, tile_cols, counts):
    blocks = vectors.shape[0]
    vecs, edge = vectors.shape[3], vectors.shape[4]
    slots = tiles.shape[2]
    row, col = lax.axis_index("row"), lax.axis_index("col")
    core = (row & 1).reshape(1)
    tiles = tiles.reshape(slots, edge, edge)
    rows, cols = tile_rows.reshape(slots), tile_cols.reshape(slots)
    live = counts.reshape(1)
    row_block, row_col = rows // AXIS, rows % AXIS
    col_block, col_row = cols // AXIS, cols % AXIS
    is_live = jnp.arange(slots, dtype=jnp.int32) < live
    mirror = is_live & (rows * AXIS + row < (col_block * AXIS + col) * AXIS + col_row)

    def row_place(step_y):
        z, inside = (col_row ^ row) >> 3, col_row & 1
        return (((step_y & 3) * 2 + z) * 2 + inside) * blocks + col_block

    def col_place(step_x, step_z):
        return ((step_x & 3) * GROUP + (step_z & 3)) * blocks + row_block

    nowhere = blocks * AXIS
    step_y = (col_row >> 1) - (row >> 1)
    step_x, step_z = row_col - col, (row_col >> 2) - (col >> 2)
    forward_source = row_place(-step_y)
    forward_target = jnp.where(is_live, col_place(step_x, step_z), nowhere)
    backward_source = col_place(-step_x, -step_z)
    backward_target = jnp.where(mirror, row_place(step_y), nowhere)
    even = core == 0
    first_source = jnp.where(even, forward_source, backward_source)
    first_target = jnp.where(even, forward_target, backward_target)
    second_source = jnp.where(even, backward_source, forward_source)
    second_target = jnp.where(even, backward_target, forward_target)

    own = vectors.reshape(blocks, vecs, edge)
    with jax.named_scope("gather_core"):
        pair = jnp.concatenate([own, send(own, to_other_core)])
    with jax.named_scope("gather_z"):
        column = jnp.concatenate([pair] + [send(pair, along_z(step)) for step in (1, 2, 3)])
    with jax.named_scope("gather_side"):
        held = [column] + [send(column, along_side(step)) for step in (1, 2, 3)]
    with jax.named_scope("gather_swap"):
        swapped = []
        for part in held:
            partner = part.reshape(GROUP, 2, blocks, vecs, edge)[:, 1].reshape(GROUP * blocks, vecs, edge)
            swapped.append(send(jnp.where(even, part[: GROUP * blocks], partner), to_other_core))
    given = multiply(True, core, first_source, first_target, live, held, tiles)
    with jax.named_scope("sum_swap"):
        got = [send(part, to_other_core) for part in given]
    kept = multiply(False, core, second_source, second_target, live, swapped, tiles)
    merged = merge(core, kept, got)
    with jax.named_scope("sum_side"):
        column = merged[0]
        for step in (1, 2, 3):
            column = column + send(merged[step], along_side(step))
    with jax.named_scope("sum_z"):
        column = column.reshape(GROUP, 2 * blocks, vecs, edge)
        pair = column[0]
        for step in (1, 2, 3):
            pair = pair + send(column[step], along_z(step))
    with jax.named_scope("sum_core"):
        result = pair[:blocks] + send(pair[blocks:], to_other_core)
    return result.reshape(blocks, 1, 1, vecs, edge)


def solution(mesh):
    in_specs = (
        P(None, "col", "row", None, None),
        P("row", "col", None, None, None),
        P("row", "col", None),
        P("row", "col", None),
        P("row", "col"),
    )
    out_specs = P(None, "col", "row", None, None)
    return jax.shard_map(shards, mesh=mesh, in_specs=in_specs, out_specs=out_specs, check_vma=False)
```

```python
import functools
import jax
import jax.numpy as jnp
from jax import lax
from jax.experimental import pallas as pl
from jax.experimental.pallas import tpu as pltpu
from jax.sharding import PartitionSpec as P

AXIS = 16
GROUP = 4
CHUNK = 8
BF16 = jnp.bfloat16
F32 = jnp.float32
AXES = ("row", "col")
SIDES = (2, 1, 3)
GSIDES = (2, 1, 3)
VECTOR = pl.BlockSpec(memory_space=pltpu.VMEM)
SCALAR = pl.BlockSpec(memory_space=pltpu.SMEM)
ANYWHERE = pl.BlockSpec(memory_space=pl.ANY)


def send(value, row_flips, col_flips):
    pairs = []
    for row in range(AXIS):
        for col in range(AXIS):
            core = row % 2
            there = (row ^ row_flips[core]) * AXIS + (col ^ col_flips[core])
            pairs.append((row * AXIS + col, there))
    return lax.ppermute(value, AXES, pairs)


def to_other_core(value):
    return send(value, (1, 1), (0, 0))


def along_z(value, step, far_step):
    return send(value, (8 if step == far_step else 2, 0), (0, 4 * step))


def along_side(value, step):
    return send(value, (2 * step, 0), (0, step))


def call(kernel, out_shape, in_specs, args, out_specs=None, scratch=(), limit=8, name=None, cost=0, aliases=None):
    return pl.pallas_call(
        kernel,
        out_shape=out_shape,
        in_specs=in_specs,
        out_specs=[VECTOR] * len(out_shape) if out_specs is None else out_specs,
        scratch_shapes=list(scratch),
        input_output_aliases=aliases or {},
        compiler_params=pltpu.CompilerParams(vmem_limit_bytes=limit * 1024 * 1024),
        cost_estimate=pl.CostEstimate(flops=0, bytes_accessed=cost, transcendentals=0),
        name=name,
    )(*args)


def is_core_0():
    return lax.axis_index("row") % 2 == 0


def stage_kernel(tiles, *refs):
    high_out, low_out = refs[-2:]

    def one_chunk(chunk, carry):
        span = pl.ds(chunk * CHUNK, CHUNK)
        tile = tiles[span]
        high = tile.astype(BF16)
        high_out[span] = high
        low_out[span] = (tile - high.astype(F32)).astype(BF16)
        return carry

    lax.fori_loop(0, tiles.shape[0] // CHUNK, one_chunk, 0)


def stage(tiles, after):
    return call(
        stage_kernel,
        [jax.ShapeDtypeStruct(tiles.shape, BF16)] * 2,
        [VECTOR] + [ANYWHERE] * len(after),
        (tiles, *after),
        name="stage",
    )


def plan(key, source, target):
    slots = key.shape[0]
    slot = jnp.arange(slots, dtype=jnp.int32)
    code = jnp.where(key < GROUP, (slot << 16) | (source << 8) | target, 0)
    before = (key[None, :] < key[:, None]) | ((key[None, :] == key[:, None]) & (slot[None, :] < slot[:, None]))
    rank = jnp.sum(before.astype(jnp.int32), axis=1)
    place = jnp.arange(128, dtype=jnp.int32)[:, None]
    ordered = jnp.where(place == rank[None, :], code[None, :], 0)
    below = jnp.where((place >= slots) & (key[None, :] < place - slots), 1, 0)
    return jnp.sum(ordered + below, axis=1).reshape(1, 128)


def plans(blocks, live, rows, cols):
    slots = rows.shape[0]
    row, col = lax.axis_index("row"), lax.axis_index("col")
    row_block, row_col = rows // AXIS, rows % AXIS
    col_block, col_row = cols // AXIS, cols % AXIS
    is_live = jnp.arange(slots, dtype=jnp.int32) < live
    mirror = is_live & (rows * AXIS + row < (col_block * AXIS + col) * AXIS + col_row)
    across, over = col_row ^ row, row_col ^ col
    row_place = (((across >> 1 & 3) * 2 + (across >> 3)) * 2 + (col_row & 1)) * blocks + col_block
    col_place = ((over & 3) * GROUP + (over >> 2)) * blocks + row_block
    even = row % 2 == 0
    first = jnp.where(even, row_place, col_place), jnp.where(even, col_place, row_place)
    second = first[1], first[0]
    first_kept = jnp.where(even, is_live, mirror)
    second_kept = jnp.where(even, mirror, is_live)
    part = GROUP * blocks
    return (
        plan(jnp.where(first_kept, first[0] // part, GROUP), *first),
        plan(jnp.where(second_kept, second[1] // part, GROUP), *second),
    )


def pair_kernel(own, other, out):
    blocks = own.shape[0]
    out[:blocks] = own[...]
    out[blocks:] = other[...]


def lift_kernel(own, out):
    out[...] = own[...]


def place_kernel(rows, cols, after, rows_out, cols_out):
    rows_out[...] = rows[...]
    cols_out[...] = cols[...]


def column_kernel(*refs):
    parts, out = refs[:GROUP], refs[-1]
    count = parts[0].shape[0]
    blocks = count // 2

    @pl.when(is_core_0())
    def _():
        for index in range(2):
            out[index * count : (index + 1) * count] = parts[index * 3][...]
        out[2 * count :] = jnp.zeros((2 * count,) + out.shape[1:], out.dtype)

    @pl.when(jnp.logical_not(is_core_0()))
    def _():
        for index, part in enumerate(parts):
            out[index * blocks : (index + 1) * blocks] = part[blocks:]
            out[2 * count + index * blocks : 2 * count + (index + 1) * blocks] = part[:blocks]


def put(split, place, values):
    vecs, edge = values.shape[1:]
    high = values.astype(BF16)
    low = (values - high.astype(F32)).astype(BF16)
    span = slice(place, place + values.shape[0])
    split[span, :vecs, :edge] = high
    split[span, :vecs, edge:] = high
    split[span, vecs:, :edge] = low
    split[span, vecs:, edge:] = low


def add_slots(transposed, bucket, plan, staged, split, total, source_mask, target_mask):
    slots = staged[0].shape[0]
    vecs = total.shape[1]
    start, end = plan[0, slots + bucket], plan[0, slots + bucket + 1]

    def one_slot(place):
        code = plan[0, place]
        slot = code >> 16
        both = jnp.concatenate([staged[0][slot], staged[1][slot]], axis=0 if transposed else 1)
        product = lax.dot_general(
            split[(code >> 8) & source_mask],
            both,
            (((1,), (0 if transposed else 1,)), ((), ())),
            preferred_element_type=F32,
        )
        target = jnp.where(place < end, code & target_mask, target_mask + 1)
        total[target] += product[:vecs] + product[vecs:]

    def one_chunk(chunk, carry):
        for step in range(CHUNK):
            one_slot(start + chunk * CHUNK + step)
        return carry

    lax.fori_loop(0, (end - start + CHUNK - 1) // CHUNK, one_chunk, 0)


def first_kernel(bucket, begin, plan, high, low, part, *refs):
    total, give, split = refs[-3:]
    count = part.shape[0] // 2
    give[...] = part[:count]
    if begin:
        total[...] = jnp.zeros_like(total)

    @pl.when(is_core_0())
    def _():
        put(split, 0, part[:count])
        add_slots(False, bucket, plan, (high, low), split, total, count - 1, GROUP * count - 1)

    @pl.when(jnp.logical_not(is_core_0()))
    def _():
        put(split, 0, part[count:])
        add_slots(True, bucket, plan, (high, low), split, total, count - 1, GROUP * count - 1)


def first(bucket, plan, staged, part, total, after):
    count, vecs, edge = part.shape[0] // 2, part.shape[1], part.shape[2]
    shape = jax.ShapeDtypeStruct((GROUP * count + 8, vecs, edge), F32)
    begin = total is None
    return call(
        functools.partial(first_kernel, bucket, begin),
        [shape, jax.ShapeDtypeStruct((count, vecs, edge), F32)],
        [SCALAR] + [VECTOR] * (3 if begin else 4) + [ANYWHERE] * len(after),
        (plan, *staged, part, *(() if begin else (total,)), *after),
        scratch=[pltpu.VMEM((count, 2 * vecs, 2 * edge), BF16)],
        aliases=None if begin else {4: 0},
        name="first",
        cost=8 << 20,
    )


def split_kernel(place, part, *refs):
    put(refs[-1], place, part[...])


def split_in(place, part, whole):
    count, vecs, edge = part.shape
    return call(
        functools.partial(split_kernel, place),
        [jax.ShapeDtypeStruct((GROUP * count, 2 * vecs, 2 * edge), BF16)],
        [VECTOR] * (1 + len(whole)),
        (part, *whole),
        aliases={1: 0} if whole else None,
        name="split",
        cost=8 << 20,
    )


def second_kernel(bucket, plan, high, low, split, got, *refs):
    out, total = refs[-2:]
    count = got.shape[0]
    blocks = count // GROUP
    total[...] = jnp.zeros_like(total)

    @pl.when(is_core_0())
    def _():
        add_slots(True, bucket, plan, (high, low), split, total, GROUP * count - 1, count - 1)
        out[:count] = total[:count] + got[...]
        out[count:] = jnp.zeros_like(got)

    @pl.when(jnp.logical_not(is_core_0()))
    def _():
        add_slots(False, bucket, plan, (high, low), split, total, GROUP * count - 1, count - 1)
        for step in range(GROUP):
            span = slice(step * blocks, (step + 1) * blocks)
            low_end = 2 * step * blocks
            out[low_end : low_end + blocks] = total[span]
            out[low_end + blocks : low_end + 2 * blocks] = got[span]


def second(bucket, plan, staged, split, got, after):
    count, vecs, edge = got.shape
    return call(
        functools.partial(second_kernel, bucket),
        [jax.ShapeDtypeStruct((2 * count, vecs, edge), F32)],
        [SCALAR] + [VECTOR] * 4 + [ANYWHERE] * len(after),
        (plan, *staged, split, got, *after),
        scratch=[pltpu.VMEM((count + 8, vecs, edge), F32)],
        name="second",
        cost=8 << 20,
    )[0]


def add_kernel(one, two, out):
    out[...] = one[...] + two[...]


def add(one, two):
    return call(add_kernel, [jax.ShapeDtypeStruct(one.shape, F32)], [VECTOR] * 2, (one, two), name="add", cost=8 << 20)[0]


def shards(vectors, tiles, tile_rows, tile_cols, counts):
    blocks = vectors.shape[0]
    vecs, edge = vectors.shape[3], vectors.shape[4]
    slots = tiles.shape[2]
    block_of = lambda count: jax.ShapeDtypeStruct((count * blocks, vecs, edge), F32)
    own = vectors.reshape(blocks, vecs, edge)
    (here,) = call(lift_kernel, [block_of(1)], [VECTOR], (own,), name="lift")
    with jax.named_scope("gather_core"):
        (pair,) = call(
            pair_kernel, [block_of(2)], [VECTOR] * 2, (here, to_other_core(own)), name="pair", cost=0
        )
    with jax.named_scope("gather_z"):
        far = [along_z(pair, step, 3) for step in (1, 2, 3)]
    staged = stage(tiles.reshape(slots, edge, edge), (pair,))
    with jax.named_scope("gather_side"):
        (column,) = call(
            column_kernel,
            [block_of(8)],
            [VECTOR] * GROUP + [ANYWHERE],
            (pair, *far, staged[0]),
            name="column",
        )
        held = {0: column}
        for step in GSIDES:
            held[step] = along_side(column, step)
    rows, cols = call(
        place_kernel,
        [jax.ShapeDtypeStruct((1, slots), jnp.int32)] * 2,
        [VECTOR] * 2 + [ANYWHERE],
        (tile_rows.reshape(1, slots), tile_cols.reshape(1, slots), column),
        name="places",
    )
    first_plan, second_plan = plans(blocks, counts.reshape(1), rows.reshape(slots), cols.reshape(slots))
    part = GROUP * blocks
    total, split, swapped = None, [], []
    for index, step in enumerate((0,) + GSIDES):
        if index >= 2:
            split = split_in(*swapped[index - 2], split)
        total, gift = first(step, first_plan, staged, held[step], total, split)
        with jax.named_scope("gather_swap"):
            swapped.append((step * part, to_other_core(gift)))
    for done in swapped[-2:]:
        split = split_in(*done, split)
    (split,) = split
    with jax.named_scope("sum_swap"):
        got = {step: to_other_core(total[step * part : (step + 1) * part]) for step in SIDES + (0,)}
    merged, after = {}, ()
    for step in SIDES + (0,):
        merged[step] = second(step, second_plan, staged, split, got[step], after)
        after = (merged[step],)
    with jax.named_scope("sum_side"):
        column = merged[0]
        for step in SIDES:
            column = add(column, along_side(merged[step], step))
    with jax.named_scope("sum_z"):
        column = column.reshape(GROUP, 2 * blocks, vecs, edge)
        pair = column[0]
        for step in (1, 2, 3):
            pair = pair + along_z(column[step], step, 1)
    with jax.named_scope("sum_core"):
        result = pair[:blocks] + to_other_core(pair[blocks:])
    return result.reshape(blocks, 1, 1, vecs, edge)


def solution(mesh):
    in_specs = (
        P(None, "col", "row", None, None),
        P("row", "col", None, None, None),
        P("row", "col", None),
        P("row", "col", None),
        P("row", "col"),
    )
    out_specs = P(None, "col", "row", None, None)
    return jax.shard_map(shards, mesh=mesh, in_specs=in_specs, out_specs=out_specs, check_vma=False)
```

```python
import functools
import jax
import jax.numpy as jnp
from jax import lax
from jax.experimental import pallas as pl
from jax.experimental.pallas import tpu as pltpu
from jax.sharding import PartitionSpec as P

AXIS = 16
GROUP = 4
CHUNK = 16
BF16 = jnp.bfloat16
F32 = jnp.float32
AXES = ("row", "col")
SIDES = (2, 1, 3)
GSIDES = (2, 1, 3)
VECTOR = pl.BlockSpec(memory_space=pltpu.VMEM)
SCALAR = pl.BlockSpec(memory_space=pltpu.SMEM)
ANYWHERE = pl.BlockSpec(memory_space=pl.ANY)


def send(value, row_flips, col_flips):
    pairs = []
    for row in range(AXIS):
        for col in range(AXIS):
            core = row % 2
            there = (row ^ row_flips[core]) * AXIS + (col ^ col_flips[core])
            pairs.append((row * AXIS + col, there))
    return lax.ppermute(value, AXES, pairs)


def to_other_core(value):
    return send(value, (1, 1), (0, 0))


def along_z(value, step, far_step):
    return send(value, (8 if step == far_step else 2, 0), (0, 4 * step))


def along_side(value, step):
    return send(value, (2 * step, 0), (0, step))


def call(kernel, out_shape, in_specs, args, out_specs=None, scratch=(), limit=8, name=None, cost=0, aliases=None):
    return pl.pallas_call(
        kernel,
        out_shape=out_shape,
        in_specs=in_specs,
        out_specs=[VECTOR] * len(out_shape) if out_specs is None else out_specs,
        scratch_shapes=list(scratch),
        input_output_aliases=aliases or {},
        compiler_params=pltpu.CompilerParams(vmem_limit_bytes=limit * 1024 * 1024),
        cost_estimate=pl.CostEstimate(flops=0, bytes_accessed=cost, transcendentals=0),
        name=name,
    )(*args)


def is_core_0():
    return lax.axis_index("row") % 2 == 0


def stage_kernel(tiles, *refs):
    high_out, low_out = refs[-2:]

    def one_chunk(chunk, carry):
        span = pl.ds(chunk * 8, 8)
        tile = tiles[span]
        high = tile.astype(BF16)
        high_out[span] = high
        low_out[span] = (tile - high.astype(F32)).astype(BF16)
        return carry

    lax.fori_loop(0, tiles.shape[0] // 8, one_chunk, 0)


def stage(tiles, after):
    return call(
        stage_kernel,
        [jax.ShapeDtypeStruct(tiles.shape, BF16)] * 2,
        [VECTOR] + [ANYWHERE] * len(after),
        (tiles, *after),
        name="stage",
    )


def plan(key, source, target):
    slots = key.shape[0]
    slot = jnp.arange(slots, dtype=jnp.int32)
    code = jnp.where(key < GROUP, (slot << 16) | (source << 8) | target, 0)
    before = (key[None, :] < key[:, None]) | ((key[None, :] == key[:, None]) & (slot[None, :] < slot[:, None]))
    rank = jnp.sum(before.astype(jnp.int32), axis=1)
    place = jnp.arange(128, dtype=jnp.int32)[:, None]
    ordered = jnp.where(place == rank[None, :], code[None, :], 0)
    below = jnp.where((place >= slots) & (key[None, :] < place - slots), 1, 0)
    return jnp.sum(ordered + below, axis=1).reshape(1, 128)


def plans(blocks, live, rows, cols):
    slots = rows.shape[0]
    row, col = lax.axis_index("row"), lax.axis_index("col")
    row_block, row_col = rows // AXIS, rows % AXIS
    col_block, col_row = cols // AXIS, cols % AXIS
    is_live = jnp.arange(slots, dtype=jnp.int32) < live
    mirror = is_live & (rows * AXIS + row < (col_block * AXIS + col) * AXIS + col_row)
    across, over = col_row ^ row, row_col ^ col
    row_place = (((across >> 1 & 3) * 2 + (across >> 3)) * 2 + (col_row & 1)) * blocks + col_block
    col_place = ((over & 3) * GROUP + (over >> 2)) * blocks + row_block
    even = row % 2 == 0
    first = jnp.where(even, row_place, col_place), jnp.where(even, col_place, row_place)
    second = first[1], first[0]
    first_kept = jnp.where(even, is_live, mirror)
    second_kept = jnp.where(even, mirror, is_live)
    part = GROUP * blocks
    return (
        plan(jnp.where(first_kept, first[0] // part, GROUP), *first),
        plan(jnp.where(second_kept, second[1] // part, GROUP), *second),
    )


def pair_kernel(own, other, out):
    blocks = own.shape[0]
    out[:blocks] = own[...]
    out[blocks:] = other[...]


def lift_kernel(own, out):
    out[...] = own[...]


def place_kernel(rows, cols, after, rows_out, cols_out):
    rows_out[...] = rows[...]
    cols_out[...] = cols[...]


def column_kernel(*refs):
    parts, out = refs[:GROUP], refs[-1]
    count = parts[0].shape[0]
    blocks = count // 2

    @pl.when(is_core_0())
    def _():
        for index in range(2):
            out[index * count : (index + 1) * count] = parts[index * 3][...]
        out[2 * count :] = jnp.zeros((2 * count,) + out.shape[1:], out.dtype)

    @pl.when(jnp.logical_not(is_core_0()))
    def _():
        for index, part in enumerate(parts):
            out[index * blocks : (index + 1) * blocks] = part[blocks:]
            out[2 * count + index * blocks : 2 * count + (index + 1) * blocks] = part[:blocks]


def put(split, place, values):
    vecs, edge = values.shape[1:]
    high = values.astype(BF16)
    low = (values - high.astype(F32)).astype(BF16)
    span = slice(place, place + values.shape[0])
    split[span, :vecs, :edge] = high
    split[span, :vecs, edge:] = high
    split[span, vecs:, :edge] = low
    split[span, vecs:, edge:] = low


def add_slots(transposed, bucket, plan, staged, split, total, source_mask, target_mask):
    slots = staged[0].shape[0]
    vecs = total.shape[1]
    start, end = plan[0, slots + bucket], plan[0, slots + bucket + 1]

    def one_slot(place):
        code = plan[0, place]
        slot = code >> 16
        both = jnp.concatenate([staged[0][slot], staged[1][slot]], axis=0 if transposed else 1)
        product = lax.dot_general(
            split[(code >> 8) & source_mask],
            both,
            (((1,), (0 if transposed else 1,)), ((), ())),
            preferred_element_type=F32,
        )
        return jnp.where(place < end, code & target_mask, target_mask + 1), product[:vecs] + product[vecs:]

    def one_chunk(chunk, carry):
        sums = [one_slot(start + chunk * CHUNK + step) for step in range(CHUNK)]
        for target, value in sums:
            total[target] += value
        return carry

    lax.fori_loop(0, (end - start + CHUNK - 1) // CHUNK, one_chunk, 0)


def first_kernel(bucket, begin, plan, high, low, part, *refs):
    total, give, split = refs[-3:]
    count = part.shape[0] // 2
    give[...] = part[:count]
    if begin:
        total[...] = jnp.zeros_like(total)

    @pl.when(is_core_0())
    def _():
        put(split, 0, part[:count])
        add_slots(False, bucket, plan, (high, low), split, total, count - 1, GROUP * count - 1)

    @pl.when(jnp.logical_not(is_core_0()))
    def _():
        put(split, 0, part[count:])
        add_slots(True, bucket, plan, (high, low), split, total, count - 1, GROUP * count - 1)


def first(bucket, plan, staged, part, total, after):
    count, vecs, edge = part.shape[0] // 2, part.shape[1], part.shape[2]
    shape = jax.ShapeDtypeStruct((GROUP * count + 8, vecs, edge), F32)
    begin = total is None
    return call(
        functools.partial(first_kernel, bucket, begin),
        [shape, jax.ShapeDtypeStruct((count, vecs, edge), F32)],
        [SCALAR] + [VECTOR] * (3 if begin else 4) + [ANYWHERE] * len(after),
        (plan, *staged, part, *(() if begin else (total,)), *after),
        scratch=[pltpu.VMEM((count, 2 * vecs, 2 * edge), BF16)],
        aliases=None if begin else {4: 0},
        name="first",
        cost=8 << 20,
    )


def split_kernel(place, part, *refs):
    put(refs[-1], place, part[...])


def split_in(place, part, whole):
    count, vecs, edge = part.shape
    return call(
        functools.partial(split_kernel, place),
        [jax.ShapeDtypeStruct((GROUP * count, 2 * vecs, 2 * edge), BF16)],
        [VECTOR] * (1 + len(whole)),
        (part, *whole),
        aliases={1: 0} if whole else None,
        name="split",
        cost=8 << 20,
    )


def second_kernel(bucket, plan, high, low, split, got, *refs):
    out, total = refs[-2:]
    count = got.shape[0]
    blocks = count // GROUP
    total[...] = jnp.zeros_like(total)

    @pl.when(is_core_0())
    def _():
        add_slots(True, bucket, plan, (high, low), split, total, GROUP * count - 1, count - 1)
        out[:count] = total[:count] + got[...]
        out[count:] = jnp.zeros_like(got)

    @pl.when(jnp.logical_not(is_core_0()))
    def _():
        add_slots(False, bucket, plan, (high, low), split, total, GROUP * count - 1, count - 1)
        for step in range(GROUP):
            span = slice(step * blocks, (step + 1) * blocks)
            low_end = 2 * step * blocks
            out[low_end : low_end + blocks] = total[span]
            out[low_end + blocks : low_end + 2 * blocks] = got[span]


def second(bucket, plan, staged, split, got, after):
    count, vecs, edge = got.shape
    return call(
        functools.partial(second_kernel, bucket),
        [jax.ShapeDtypeStruct((2 * count, vecs, edge), F32)],
        [SCALAR] + [VECTOR] * 4 + [ANYWHERE] * len(after),
        (plan, *staged, split, got, *after),
        scratch=[pltpu.VMEM((count + 8, vecs, edge), F32)],
        name="second",
        cost=8 << 20,
    )[0]


def add_kernel(one, two, out):
    out[...] = one[...] + two[...]


def add(one, two):
    return call(add_kernel, [jax.ShapeDtypeStruct(one.shape, F32)], [VECTOR] * 2, (one, two), name="add", cost=8 << 20)[0]


def shards(vectors, tiles, tile_rows, tile_cols, counts):
    blocks = vectors.shape[0]
    vecs, edge = vectors.shape[3], vectors.shape[4]
    slots = tiles.shape[2]
    block_of = lambda count: jax.ShapeDtypeStruct((count * blocks, vecs, edge), F32)
    own = vectors.reshape(blocks, vecs, edge)
    (here,) = call(lift_kernel, [block_of(1)], [VECTOR], (own,), name="lift")
    with jax.named_scope("gather_core"):
        (pair,) = call(
            pair_kernel, [block_of(2)], [VECTOR] * 2, (here, to_other_core(own)), name="pair", cost=0
        )
    with jax.named_scope("gather_z"):
        far = [along_z(pair, step, 3) for step in (1, 2, 3)]
    staged = stage(tiles.reshape(slots, edge, edge), (pair,))
    with jax.named_scope("gather_side"):
        (column,) = call(
            column_kernel,
            [block_of(8)],
            [VECTOR] * GROUP + [ANYWHERE],
            (pair, *far, staged[0]),
            name="column",
        )
        held = {0: column}
        for step in GSIDES:
            held[step] = along_side(column, step)
    rows, cols = call(
        place_kernel,
        [jax.ShapeDtypeStruct((1, slots), jnp.int32)] * 2,
        [VECTOR] * 2 + [ANYWHERE],
        (tile_rows.reshape(1, slots), tile_cols.reshape(1, slots), column),
        name="places",
    )
    first_plan, second_plan = plans(blocks, counts.reshape(1), rows.reshape(slots), cols.reshape(slots))
    part = GROUP * blocks
    total, split, swapped = None, [], []
    for index, step in enumerate((0,) + GSIDES):
        if index >= 2:
            split = split_in(*swapped[index - 2], split)
        total, gift = first(step, first_plan, staged, held[step], total, split)
        with jax.named_scope("gather_swap"):
            swapped.append((step * part, to_other_core(gift)))
    for done in swapped[-2:]:
        split = split_in(*done, split)
    (split,) = split
    with jax.named_scope("sum_swap"):
        got = {step: to_other_core(total[step * part : (step + 1) * part]) for step in SIDES + (0,)}
    merged, after = {}, ()
    for step in SIDES + (0,):
        merged[step] = second(step, second_plan, staged, split, got[step], after)
        after = (merged[step],)
    with jax.named_scope("sum_side"):
        column = merged[0]
        for step in SIDES:
            column = add(column, along_side(merged[step], step))
    with jax.named_scope("sum_z"):
        column = column.reshape(GROUP, 2 * blocks, vecs, edge)
        pair = column[0]
        for step in (1, 2, 3):
            pair = pair + along_z(column[step], step, 1)
    with jax.named_scope("sum_core"):
        result = pair[:blocks] + to_other_core(pair[blocks:])
    return result.reshape(blocks, 1, 1, vecs, edge)


def solution(mesh):
    in_specs = (
        P(None, "col", "row", None, None),
        P("row", "col", None, None, None),
        P("row", "col", None),
        P("row", "col", None),
        P("row", "col"),
    )
    out_specs = P(None, "col", "row", None, None)
    return jax.shard_map(shards, mesh=mesh, in_specs=in_specs, out_specs=out_specs, check_vma=False)
```

```python
import functools
import jax
import jax.numpy as jnp
from jax import lax
from jax.experimental import pallas as pl
from jax.experimental.pallas import tpu as pltpu
from jax.sharding import PartitionSpec as P

AXIS = 16
GROUP = 4
CHUNK = 16
BF16 = jnp.bfloat16
F32 = jnp.float32
AXES = ("row", "col")
SIDES = (2, 3, 1)
GSIDES = (2, 1, 3)
VECTOR = pl.BlockSpec(memory_space=pltpu.VMEM)
SCALAR = pl.BlockSpec(memory_space=pltpu.SMEM)
ANYWHERE = pl.BlockSpec(memory_space=pl.ANY)


def send(value, row_flips, col_flips):
    pairs = []
    for row in range(AXIS):
        for col in range(AXIS):
            core = row % 2
            there = (row ^ row_flips[core]) * AXIS + (col ^ col_flips[core])
            pairs.append((row * AXIS + col, there))
    return lax.ppermute(value, AXES, pairs)


def to_other_core(value):
    return send(value, (1, 1), (0, 0))


def along_z(value, step, far_step):
    return send(value, (8 if step == far_step else 2, 0), (0, 4 * step))


def along_side(value, step):
    return send(value, (2 * step, 0), (0, step))


def call(kernel, out_shape, in_specs, args, out_specs=None, scratch=(), limit=8, name=None, cost=0, aliases=None):
    return pl.pallas_call(
        kernel,
        out_shape=out_shape,
        in_specs=in_specs,
        out_specs=[VECTOR] * len(out_shape) if out_specs is None else out_specs,
        scratch_shapes=list(scratch),
        input_output_aliases=aliases or {},
        compiler_params=pltpu.CompilerParams(vmem_limit_bytes=limit * 1024 * 1024),
        cost_estimate=pl.CostEstimate(flops=0, bytes_accessed=cost, transcendentals=0),
        name=name,
    )(*args)


def is_core_0():
    return lax.axis_index("row") % 2 == 0


def stage_kernel(tiles, *refs):
    high_out, low_out = refs[-2:]

    def one_chunk(chunk, carry):
        span = pl.ds(chunk * 8, 8)
        tile = tiles[span]
        high = tile.astype(BF16)
        high_out[span] = high
        low_out[span] = (tile - high.astype(F32)).astype(BF16)
        return carry

    lax.fori_loop(0, tiles.shape[0] // 8, one_chunk, 0)


def stage(tiles, after):
    return call(
        stage_kernel,
        [jax.ShapeDtypeStruct(tiles.shape, BF16)] * 2,
        [VECTOR] + [ANYWHERE] * len(after),
        (tiles, *after),
        name="stage",
    )


def plan(key, source, target):
    slots = key.shape[0]
    slot = jnp.arange(slots, dtype=jnp.int32)
    code = jnp.where(key < GROUP, (slot << 16) | (source << 8) | target, 0)
    before = (key[None, :] < key[:, None]) | ((key[None, :] == key[:, None]) & (slot[None, :] < slot[:, None]))
    rank = jnp.sum(before.astype(jnp.int32), axis=1)
    place = jnp.arange(128, dtype=jnp.int32)[:, None]
    ordered = jnp.where(place == rank[None, :], code[None, :], 0)
    below = jnp.where((place >= slots) & (key[None, :] < place - slots), 1, 0)
    return jnp.sum(ordered + below, axis=1).reshape(1, 128)


def plans(blocks, live, rows, cols):
    slots = rows.shape[0]
    row, col = lax.axis_index("row"), lax.axis_index("col")
    row_block, row_col = rows // AXIS, rows % AXIS
    col_block, col_row = cols // AXIS, cols % AXIS
    is_live = jnp.arange(slots, dtype=jnp.int32) < live
    mirror = is_live & (rows * AXIS + row < (col_block * AXIS + col) * AXIS + col_row)
    across, over = col_row ^ row, row_col ^ col
    row_place = (((across >> 1 & 3) * 2 + (across >> 3)) * 2 + (col_row & 1)) * blocks + col_block
    col_place = ((over & 3) * GROUP + (over >> 2)) * blocks + row_block
    even = row % 2 == 0
    first = jnp.where(even, row_place, col_place), jnp.where(even, col_place, row_place)
    second = first[1], first[0]
    first_kept = jnp.where(even, is_live, mirror)
    second_kept = jnp.where(even, mirror, is_live)
    part = GROUP * blocks
    return (
        plan(jnp.where(first_kept, first[0] // part, GROUP), *first),
        plan(jnp.where(second_kept, second[1] // part, GROUP), *second),
    )


def pair_kernel(own, other, out):
    blocks = own.shape[0]
    out[:blocks] = own[...]
    out[blocks:] = other[...]


def lift_kernel(own, out):
    out[...] = own[...]


def place_kernel(rows, cols, after, rows_out, cols_out):
    rows_out[...] = rows[...]
    cols_out[...] = cols[...]


def column_kernel(*refs):
    parts, out = refs[:GROUP], refs[-1]
    count = parts[0].shape[0]
    blocks = count // 2

    @pl.when(is_core_0())
    def _():
        for index in range(2):
            out[index * count : (index + 1) * count] = parts[index * 3][...]
        out[2 * count :] = jnp.zeros((2 * count,) + out.shape[1:], out.dtype)

    @pl.when(jnp.logical_not(is_core_0()))
    def _():
        for index, part in enumerate(parts):
            out[index * blocks : (index + 1) * blocks] = part[blocks:]
            out[2 * count + index * blocks : 2 * count + (index + 1) * blocks] = part[:blocks]


def put(split, place, values):
    vecs, edge = values.shape[1:]
    high = values.astype(BF16)
    low = (values - high.astype(F32)).astype(BF16)
    span = slice(place, place + values.shape[0])
    split[span, :vecs, :edge] = high
    split[span, :vecs, edge:] = high
    split[span, vecs:, :edge] = low
    split[span, vecs:, edge:] = low


def add_slots(transposed, bucket, plan, staged, split, total, source_mask, target_mask):
    slots = staged[0].shape[0]
    vecs = total.shape[1]
    start, end = plan[0, slots + bucket], plan[0, slots + bucket + 1]

    def one_slot(place):
        code = plan[0, place]
        slot = code >> 16
        both = jnp.concatenate([staged[0][slot], staged[1][slot]], axis=0 if transposed else 1)
        product = lax.dot_general(
            split[(code >> 8) & source_mask],
            both,
            (((1,), (0 if transposed else 1,)), ((), ())),
            preferred_element_type=F32,
        )
        return jnp.where(place < end, code & target_mask, target_mask + 1), product[:vecs] + product[vecs:]

    def one_chunk(chunk, carry):
        sums = [one_slot(start + chunk * CHUNK + step) for step in range(CHUNK)]
        for target, value in sums:
            total[target] += value
        return carry

    lax.fori_loop(0, (end - start + CHUNK - 1) // CHUNK, one_chunk, 0)


def first_kernel(bucket, begin, plan, high, low, part, *refs):
    total, give, split = refs[-3:]
    count = part.shape[0] // 2
    give[...] = part[:count]
    if begin:
        total[...] = jnp.zeros_like(total)

    @pl.when(is_core_0())
    def _():
        put(split, 0, part[:count])
        add_slots(False, bucket, plan, (high, low), split, total, count - 1, GROUP * count - 1)

    @pl.when(jnp.logical_not(is_core_0()))
    def _():
        put(split, 0, part[count:])
        add_slots(True, bucket, plan, (high, low), split, total, count - 1, GROUP * count - 1)


def first(bucket, plan, staged, part, total, after):
    count, vecs, edge = part.shape[0] // 2, part.shape[1], part.shape[2]
    shape = jax.ShapeDtypeStruct((GROUP * count + 8, vecs, edge), F32)
    begin = total is None
    return call(
        functools.partial(first_kernel, bucket, begin),
        [shape, jax.ShapeDtypeStruct((count, vecs, edge), F32)],
        [SCALAR] + [VECTOR] * (3 if begin else 4) + [ANYWHERE] * len(after),
        (plan, *staged, part, *(() if begin else (total,)), *after),
        scratch=[pltpu.VMEM((count, 2 * vecs, 2 * edge), BF16)],
        aliases=None if begin else {4: 0},
        name="first",
        cost=8 << 20,
    )


def split_kernel(place, part, *refs):
    put(refs[-1], place, part[...])


def split_in(place, part, whole):
    count, vecs, edge = part.shape
    return call(
        functools.partial(split_kernel, place),
        [jax.ShapeDtypeStruct((GROUP * count, 2 * vecs, 2 * edge), BF16)],
        [VECTOR] * (1 + len(whole)),
        (part, *whole),
        aliases={1: 0} if whole else None,
        name="split",
        cost=8 << 20,
    )


def second_kernel(bucket, plan, high, low, split, got, *refs):
    out, total = refs[-2:]
    count = got.shape[0]
    blocks = count // GROUP
    total[...] = jnp.zeros_like(total)

    @pl.when(is_core_0())
    def _():
        add_slots(True, bucket, plan, (high, low), split, total, GROUP * count - 1, count - 1)
        out[:count] = total[:count] + got[...]
        out[count:] = jnp.zeros_like(got)

    @pl.when(jnp.logical_not(is_core_0()))
    def _():
        add_slots(False, bucket, plan, (high, low), split, total, GROUP * count - 1, count - 1)
        for step in range(GROUP):
            span = slice(step * blocks, (step + 1) * blocks)
            low_end = 2 * step * blocks
            out[low_end : low_end + blocks] = total[span]
            out[low_end + blocks : low_end + 2 * blocks] = got[span]


def second(bucket, plan, staged, split, got, after):
    count, vecs, edge = got.shape
    return call(
        functools.partial(second_kernel, bucket),
        [jax.ShapeDtypeStruct((2 * count, vecs, edge), F32)],
        [SCALAR] + [VECTOR] * 4 + [ANYWHERE] * len(after),
        (plan, *staged, split, got, *after),
        scratch=[pltpu.VMEM((count + 8, vecs, edge), F32)],
        name="second",
        cost=8 << 20,
    )[0]


def add_kernel(one, two, out):
    out[...] = one[...] + two[...]


def add(one, two):
    return call(add_kernel, [jax.ShapeDtypeStruct(one.shape, F32)], [VECTOR] * 2, (one, two), name="add", cost=8 << 20)[0]


def shards(vectors, tiles, tile_rows, tile_cols, counts):
    blocks = vectors.shape[0]
    vecs, edge = vectors.shape[3], vectors.shape[4]
    slots = tiles.shape[2]
    block_of = lambda count: jax.ShapeDtypeStruct((count * blocks, vecs, edge), F32)
    own = vectors.reshape(blocks, vecs, edge)
    (here,) = call(lift_kernel, [block_of(1)], [VECTOR], (own,), name="lift")
    with jax.named_scope("gather_core"):
        (pair,) = call(
            pair_kernel, [block_of(2)], [VECTOR] * 2, (here, to_other_core(own)), name="pair", cost=0
        )
    with jax.named_scope("gather_z"):
        far = [along_z(pair, step, 3) for step in (1, 2, 3)]
    staged = stage(tiles.reshape(slots, edge, edge), (pair,))
    with jax.named_scope("gather_side"):
        (column,) = call(
            column_kernel,
            [block_of(8)],
            [VECTOR] * GROUP,
            (pair, *far),
            name="column",
        )
        held = {0: column}
        for step in GSIDES:
            held[step] = along_side(column, step)
    rows, cols = call(
        place_kernel,
        [jax.ShapeDtypeStruct((1, slots), jnp.int32)] * 2,
        [VECTOR] * 2 + [ANYWHERE],
        (tile_rows.reshape(1, slots), tile_cols.reshape(1, slots), column),
        name="places",
    )
    first_plan, second_plan = plans(blocks, counts.reshape(1), rows.reshape(slots), cols.reshape(slots))
    part = GROUP * blocks
    total, split, swapped = None, [], []
    for index, step in enumerate((0,) + GSIDES):
        if index >= 2:
            split = split_in(*swapped[index - 2], split)
        total, gift = first(step, first_plan, staged, held[step], total, split)
        with jax.named_scope("gather_swap"):
            swapped.append((step * part, to_other_core(gift)))
    for done in swapped[-2:]:
        split = split_in(*done, split)
    (split,) = split
    with jax.named_scope("sum_swap"):
        got = {step: to_other_core(total[step * part : (step + 1) * part]) for step in SIDES + (0,)}
    merged, after = {}, ()
    for step in SIDES + (0,):
        merged[step] = second(step, second_plan, staged, split, got[step], after)
        after = (merged[step],)
    with jax.named_scope("sum_side"):
        column = merged[0]
        for step in SIDES:
            column = add(column, along_side(merged[step], step))
    with jax.named_scope("sum_z"):
        column = column.reshape(GROUP, 2 * blocks, vecs, edge)
        pair = column[0]
        for step in (1, 2, 3):
            pair = pair + along_z(column[step], step, 1)
    with jax.named_scope("sum_core"):
        result = pair[:blocks] + to_other_core(pair[blocks:])
    return result.reshape(blocks, 1, 1, vecs, edge)


def solution(mesh):
    in_specs = (
        P(None, "col", "row", None, None),
        P("row", "col", None, None, None),
        P("row", "col", None),
        P("row", "col", None),
        P("row", "col"),
    )
    out_specs = P(None, "col", "row", None, None)
    return jax.shard_map(shards, mesh=mesh, in_specs=in_specs, out_specs=out_specs, check_vma=False)
```
